512 devices in a mesh: site: 32 (over z, core), sector: 16 (over y, x).
Axes of the slice: x: 4, y: 4, z: 16, core: 2. Of those that a mesh axis runs over, the one named last changes fastest.
Arguments:
- site_tensors: bfloat16 [64, 32, 4, 128, 128], P('site', 'sector'), may hold values from -0.375 to 0.375
- charge_step: int32 [64, 4], P('site'), may hold values from -2 to 2, as said below
- local_operator: bfloat16 [13, 13, 4], replicated, may hold values from -1.75 to 1.75
- left_boundary: bfloat16 [32, 32, 13, 128, 128], P('site', 'sector'), may hold values from -6 to 6
- right_boundary: bfloat16 [32, 32, 13, 128, 128], P('site', 'sector'), may hold values from -6 to 6
Outputs:
- new_left: bfloat16 [32, 32, 13, 128, 128], P('site', 'sector')
- new_right: bfloat16 [32, 32, 13, 128, 128], P('site', 'sector')
The draws below stay inside these ranges and needn't reach their ends.
Inputs may be any that keep to these rules, and one draw needn't show every extreme that they name: `charge_step`: at every site one local state shifts the sector label by 2 and another by -2.
All inputs are finite; a program needn't handle non-finite values.
Results may differ from the reference program's by a relative error of at most 0.011.
Values may be sent and summed in bfloat16 or wider, within the bound.
A program may use at most 64 MiB of HBM per device.

```python
import jax
import jax.numpy as jnp
from jax import lax

BS = 128
WMPO = 13
D_PHYS = 4
SITE_DEV = 2
SEC_DEV = 2
NSEC = 32
NSEG = 32
NSITES = 64
N_SECTOR = 16


def draw_charge_step(key, part):
    first_key = jax.random.fold_in(key, 11)
    second_key = jax.random.fold_in(key, 23)
    third_key = jax.random.fold_in(key, 37)
    values = jax.random.randint(first_key, (NSITES, D_PHYS), 0 - SEC_DEV, SEC_DEV + 1).astype(jnp.int32)
    upper_state = jax.random.randint(second_key, (NSITES, 1), 0, D_PHYS).astype(jnp.int32)
    offset = jax.random.randint(third_key, (NSITES, 1), 1, D_PHYS).astype(jnp.int32)
    lower_state = (upper_state + offset) % D_PHYS
    states = lax.broadcasted_iota(jnp.int32, (NSITES, D_PHYS), 1)
    values = jnp.where(states == upper_state, SEC_DEV, values)
    values = jnp.where(states == lower_state, 0 - SEC_DEV, values)
    return values.astype(jnp.int32)


def block_scale(rng, extent, shards, least, largest):
    loudness = 1.0
    for dim, blocks in shards:
        draws = jax.random.uniform(jax.random.fold_in(jax.random.fold_in(rng, 6), dim), (blocks,), jnp.float32, least / len(shards), largest / len(shards))
        loudness = loudness * jnp.repeat(jnp.exp(draws), extent[dim] // blocks).reshape((-1,) + (1,) * (len(extent) - 1 - dim))
    return loudness


def centred(stream_key, extent, width, reach, cuts=(), held_as=jnp.bfloat16):
    level = block_scale(stream_key, extent, cuts, -0.22, 0.18) if cuts else 1.0
    drawn = jax.random.normal(stream_key, extent, jnp.float32) * width * level
    return jnp.minimum(jnp.maximum(drawn, -reach), reach).astype(held_as)


def setup_inputs(seed: int = 0) -> dict:
    keys = jax.random.split(jax.random.key(seed), 6)
    site_tensors = centred(keys[0], (NSITES, NSEC, D_PHYS, BS, BS), (2 * BS) ** -0.5, 0.375, ((0, 32), (1, 16)))
    charge_step = draw_charge_step(jax.random.fold_in(keys[5], 71), 0)
    local_operator = centred(keys[2], (WMPO, WMPO, D_PHYS), WMPO ** -0.5, 1.75)
    left_boundary = centred(keys[3], (NSEG, NSEC, WMPO, BS, BS), 1.0, 6.0, ((0, 32), (1, 16)))
    right_boundary = centred(keys[4], (NSEG, NSEC, WMPO, BS, BS), 1.0, 6.0, ((0, 32), (1, 16)))
    return {"site_tensors": site_tensors, "charge_step": charge_step, "local_operator": local_operator, "left_boundary": left_boundary, "right_boundary": right_boundary}


def sector_targets(steps):
    labels = lax.broadcasted_iota(jnp.int32, (D_PHYS, NSEC), 1)
    return ((labels + steps.astype(jnp.int32)[:, None]) % NSEC).astype(jnp.int32)


def left_update(environ, tensors, steps, operator_terms):
    targets = sector_targets(steps)
    product = jnp.einsum('iwab,isbc->iswac', environ.astype(jnp.float32), tensors.astype(jnp.float32))
    product = lax.optimization_barrier(product.astype(jnp.bfloat16)).astype(jnp.float32)
    mixture = jnp.einsum('iswac,wvs->isvac', product, operator_terms.astype(jnp.float32)).astype(jnp.bfloat16)
    contrib = jnp.einsum('isbc,isvbd->isvcd', tensors.astype(jnp.float32), mixture.astype(jnp.float32))
    group_terms = contrib.reshape((N_SECTOR, SEC_DEV * D_PHYS) + contrib.shape[2:])
    target_rows = jnp.transpose(targets).reshape(N_SECTOR, SEC_DEV * D_PHYS).astype(jnp.int32)

    def one_group(total, group_items):
        block_terms, group_index = group_items
        group_share = jax.ops.segment_sum(block_terms, group_index, num_segments=NSEC)
        rounded = lax.optimization_barrier(group_share.astype(jnp.bfloat16)).astype(jnp.float32)
        return total + rounded, None

    start_total = jnp.zeros((NSEC,) + contrib.shape[2:], jnp.float32)
    total, unused = lax.scan(one_group, start_total, (group_terms, target_rows))
    return total.astype(jnp.bfloat16)


def right_update(environ, tensors, steps, operator_terms):
    targets = sector_targets(steps)
    picked = environ[jnp.transpose(targets).astype(jnp.int32)]
    folded = jnp.einsum('isvab,wvs->iswab', picked.astype(jnp.float32), operator_terms.astype(jnp.float32)).astype(jnp.bfloat16)
    half_prod = jnp.einsum('isac,iswcd->iswad', tensors.astype(jnp.float32), folded.astype(jnp.float32)).astype(jnp.bfloat16)
    return jnp.einsum('iswad,isbd->iwab', half_prod.astype(jnp.float32), tensors.astype(jnp.float32)).astype(jnp.bfloat16)


def reference(site_tensors, charge_step, local_operator, left_boundary, right_boundary):
    zero_block = jnp.zeros_like(left_boundary[:1])
    left_in = jnp.concatenate([zero_block, left_boundary[:-1]], axis=0)
    right_in = jnp.concatenate([right_boundary[1:], zero_block], axis=0)
    site_pairs = site_tensors.reshape((NSEG, SITE_DEV) + site_tensors.shape[1:])
    step_pairs = charge_step.reshape((NSEG, SITE_DEV, D_PHYS))

    def segment(segment_items):
        left_env, right_env, tensors, steps = segment_items
        mid_left = left_update(left_env, tensors[0], steps[0], local_operator)
        out_left = left_update(mid_left, tensors[1], steps[1], local_operator)
        mid_right = right_update(right_env, tensors[1], steps[1], local_operator)
        out_right = right_update(mid_right, tensors[0], steps[0], local_operator)
        return out_left, out_right

    new_left, new_right = lax.map(segment, (left_in, right_in, site_pairs, step_pairs))
    return new_left, new_right
```

```python
import functools

import jax
import jax.numpy as jnp
from jax import lax
from jax.experimental import pallas as pl
from jax.experimental.pallas import tpu as pltpu
from jax.sharding import PartitionSpec as P

MESH = pl.DeviceIdType.MESH
BF = jnp.bfloat16
F32 = jnp.float32
W = 13
S = 4
BS = 128
R = 16
KW = W * R


def dot(a, b):
    return jnp.dot(a, b, preferred_element_type=F32)


def dot_nt(a, b):
    return lax.dot_general(a, b, (((1,), (1,)), ((), ())), preferred_element_type=F32)


def kernel(
    zs, steps_in, op_ref, m_in, left_in, right_in, left_out, right_out,
    tens, win1, win2, land, shr, res, own, prod, mix, kron, mt, steps_v, steps_s,
    st_send, st_recv, m_send, m_recv, e_send, e_recv, x_send, x_recv, o_send, o_recv, loc,
):
    site = lax.axis_index("site")
    sector = lax.axis_index("sector")
    z, c = site // 2, site % 2
    y, x = sector // 4, sector % 4
    half = x // 2
    slot = x % 2
    home = half == c
    is_right = (x == 0) | (x == 3)
    is_left = jnp.logical_not(is_right)

    def dev(zz, cc, yy, xx):
        return (zz * 2 + cc, yy * 4 + xx)

    def signal(sem, target):
        pl.semaphore_signal(sem, inc=1, device_id=target, device_id_type=MESH)

    left_task = dev(z, half, y, 1 + c)
    right_task = dev(z, half, y, 3 * c)
    left_next = dev(z + c, half, y, 2 - c)
    right_next = dev(z + c - 1, half, y, 3 - 3 * c)
    has_left_next = z + c < zs
    has_right_next = z + c - 1 >= 0
    src = [dev(z, half, y, 2 * c + k) for k in range(2)]
    away = half - 1 + is_right.astype(jnp.int32)
    fed = (z + away >= 0) & (z + away < zs)
    env_src = [dev(z + away, 1 - half, y, 2 * c + k) for k in range(2)]
    down = dev(z, 1 - c, (y + c + 3) % 4, x)
    up = dev(z, 1 - c, (y + c) % 4, x)

    barrier = pltpu.get_barrier_semaphore()
    for k in range(2):
        pl.when(jnp.logical_not(home & (slot == k)))(functools.partial(signal, barrier, src[k]))
        pl.when(fed)(functools.partial(signal, barrier, env_src[k]))
    pl.when(x != 1 + c)(functools.partial(signal, barrier, left_task))
    pl.when(x != 3 * c)(functools.partial(signal, barrier, right_task))
    signal(barrier, down)
    signal(barrier, up)
    pl.semaphore_wait(
        barrier,
        6
        - 2 * home.astype(jnp.int32)
        + has_left_next.astype(jnp.int32)
        + has_right_next.astype(jnp.int32),
    )

    def remote(a, b, ss, rs, target):
        return pltpu.make_async_remote_copy(
            src_ref=a, dst_ref=b, send_sem=ss, recv_sem=rs, device_id=target, device_id_type=MESH
        )

    def push(a, b, ss, rs, target, here):
        @pl.when(here)
        def _():
            pltpu.make_async_copy(a, b, rs).start()

        @pl.when(jnp.logical_not(here))
        def _():
            remote(a, b, ss, rs, target).start()

    def pushed(a, b, ss, rs, target, here):
        @pl.when(jnp.logical_not(here))
        def _():
            remote(a, b, ss, rs, target).wait_send()

    def arrived(b, rs):
        pltpu.make_async_copy(b, b, rs).wait()

    tasks = ((left_task, x == 1 + c), (right_task, x == 3 * c))

    def steps_args(t):
        return (steps_in, steps_v.at[slot], st_send.at[t], st_recv.at[slot]) + tasks[t]

    def m_args(t, k):
        return (
            m_in.at[k], tens.at[k, pl.ds(2 * slot, 2)], m_send.at[t, k], m_recv.at[k, slot]
        ) + tasks[t]

    def env_copy(t):
        held, target = ((left_in, left_next), (right_in, right_next))[t]
        return remote(
            held.at[0], win1.at[pl.ds(2 + 2 * slot, 2)], e_send.at[t], e_recv.at[slot], target
        )

    has_next = (has_left_next, has_right_next)
    for t in range(2):
        push(*steps_args(t))
    for t in range(2):
        push(*m_args(t, t))
        pl.when(has_next[t])(lambda t=t: env_copy(t).start())
    for t in range(2):
        push(*m_args(t, 1 - t))

    @pl.when(jnp.logical_not(fed))
    def _():
        win1[2:6] = jnp.zeros((4, W, BS, BS), BF)

    rows = lax.broadcasted_iota(jnp.int32, (KW, R), 0)
    cols = lax.broadcasted_iota(jnp.int32, (KW, R), 1)
    spread = (rows // R == cols).astype(F32).astype(BF)
    by_row = dot(spread, op_ref[...]).astype(BF)
    rows = lax.broadcasted_iota(jnp.int32, (KW, BS), 0)
    cols = lax.broadcasted_iota(jnp.int32, (KW, BS), 1)
    place_row = lax.broadcasted_iota(jnp.int32, (KW, KW), 0) % R
    place_col = lax.broadcasted_iota(jnp.int32, (KW, KW), 1) % R
    for s in range(S):
        pick = ((rows // R) * S + s == cols).astype(F32).astype(BF)

        @pl.when(is_left)
        def _():
            full = dot_nt(pick, by_row)
            kron[s] = jnp.where(place_row == place_col, full, 0.0).astype(BF)

        @pl.when(is_right)
        def _():
            full = dot_nt(by_row, pick)
            kron[s] = jnp.where(place_row == place_col, full, 0.0).astype(BF)

    for k in range(2):
        arrived(steps_v.at[k], st_recv.at[k])
    fetch = pltpu.make_async_copy(steps_v.at[0], steps_s, loc)
    fetch.start()
    fetch.wait()

    outer = c
    inner = 1 - c

    def wait_env(g):
        @pl.when(fed)
        def _():
            arrived(win1.at[pl.ds(2 + 2 * g, 2)], e_recv.at[g])

    def wait_m(k, g):
        arrived(tens.at[k, pl.ds(2 * g, 2)], m_recv.at[k, g])

    def swap_send(a, k, g):
        @pl.when(g == 0)
        def _():
            remote(a, land.at[k, 1], x_send.at[k, 0], x_recv.at[k, 1], down).start()

        @pl.when(g == 1)
        def _():
            remote(a, land.at[k, 0], x_send.at[k, 1], x_recv.at[k, 0], up).start()

    def wait_land(k, g):
        arrived(land.at[k, g], x_recv.at[k, g])

    def out_args(g, target_ref, t):
        here = home & (slot == g)
        return (
            res.at[pl.ds(2 * g, 2)], target_ref.at[0], o_send.at[g], o_recv.at[t],
            dev(z, half, y, 2 * c + g), here,
        )

    def blend(load, store):
        for s in range(S):
            for a in range(0, BS // R, 2):
                both = jnp.concatenate([load(s, a), load(s, a + 1)], axis=1)
                r = dot(kron[s], both).astype(BF)
                store(s, a, r[:, :BS].reshape(W, R, BS))
                store(s, a + 1, r[:, BS:].reshape(W, R, BS))

    @pl.when(is_left)
    def _():
        mt[4] = jnp.zeros((S, BS, BS), BF)

        def flip(k, g):
            def body(n, carry):
                i = 2 * g + n
                for s in range(S):
                    mt[i, s] = tens[k, i, s].astype(F32).T.astype(BF)
                return carry

            lax.fori_loop(0, 2, body, 0)

        def expand(k, win, g):
            def body(n, carry):
                i = 2 * g + n
                for p in range(2):
                    m = jnp.concatenate([tens[k, i, 2 * p], tens[k, i, 2 * p + 1]], axis=1)
                    r = dot(win[2 + i].reshape(W * BS, BS), m).astype(BF)
                    prod[p] = r.reshape(W, BS, 2 * BS)

                def load(s, a):
                    block = prod[s // 2, :, a * R : (a + 1) * R, (s % 2) * BS : (s % 2 + 1) * BS]
                    return block.reshape(KW, BS)

                def store(s, a, r):
                    mix[i, s, :, a * R : (a + 1) * R, :] = r

                blend(load, store)
                return carry

            lax.fori_loop(0, 2, body, 0)

        def reach(k, j, low, high, put):
            origin = [j - steps_s[k, s] for s in range(S)]
            inside = [(i >= low) & (i <= high) for i in origin]
            clipped = [jnp.minimum(jnp.maximum(i, low), high) for i in origin]
            lhs = jnp.concatenate(
                [mt[jnp.where(inside[s], clipped[s], 4), s] for s in range(S)], axis=1
            )
            for v0 in range(0, W, 2):
                vs = range(v0, min(v0 + 2, W))
                rhs = jnp.concatenate(
                    [
                        jnp.concatenate([mix[clipped[s], s, v] for s in range(S)], axis=0)
                        for v in vs
                    ],
                    axis=1,
                )
                r = dot(lhs, rhs).astype(BF)
                for n, v in enumerate(vs):
                    put(v, r[:, n * BS : (n + 1) * BS])

        def share(k, g):
            def body(n, carry):
                def put(v, r):
                    shr[k, g, n, v] = r

                reach(k, 6 * g - 2 + n, 2 * g, 2 * g + 1, put)
                return carry

            lax.fori_loop(0, 2, body, 0)
            swap_send(shr.at[k, g], k, g)

        def settle(k):
            def body(j, carry):
                def put(v, r):
                    own[j, v] = r

                reach(k, j, 0, 3, put)
                return carry

            lax.fori_loop(0, 4, body, 0)

        def join(k, g, put):
            wait_land(k, g)

            def body(n, carry):
                j = 2 * g + n
                put(j, (own[j].astype(F32) + land[k, g, n].astype(F32)).astype(BF))
                return carry

            lax.fori_loop(0, 2, body, 0)

        def put_mid(j, r):
            win2[2 + j] = r

        def put_res(j, r):
            res[j] = r

        for g in (outer, inner):
            wait_m(0, g)
            flip(0, g)
            wait_env(g)
            expand(0, win1, g)
            share(0, g)
        settle(0)
        for g in (inner, outer):
            wait_m(1, g)
            flip(1, g)
            join(0, g, put_mid)
            expand(1, win2, g)
            share(1, g)
        settle(1)
        for g in (inner, outer):
            join(1, g, put_res)
            push(*out_args(g, left_out, 0))
        for g in (inner, outer):
            pushed(*out_args(g, left_out, 0))
        for k in range(2):
            for g in range(2):
                remote(
                    shr.at[k, g], land.at[k, 1 - g], x_send.at[k, g], x_recv.at[k, 1 - g], up
                ).wait_send()

    @pl.when(is_right)
    def _():
        def widen(k, win, g):
            wait_land(k, g)
            win[pl.ds(6 * g, 2)] = land[k, g]

        def update(k, win, g, put):
            def body(n, carry):
                i = 2 * g + n
                at = [2 + i + steps_s[k, s] for s in range(S)]

                def load(s, a):
                    return win[at[s], :, a * R : (a + 1) * R, :].reshape(KW, BS)

                def store(s, a, r):
                    mix[0, s, :, a * R : (a + 1) * R, :] = r

                blend(load, store)
                for s in range(S):
                    for w0 in range(0, W, 2):
                        ws = range(w0, min(w0 + 2, W))
                        rhs = jnp.concatenate([mix[0, s, w] for w in ws], axis=1)
                        r = dot(tens[k, i, s], rhs).astype(BF)
                        for m, w in enumerate(ws):
                            prod[s // 2, w, :, (s % 2) * BS : (s % 2 + 1) * BS] = r[
                                :, m * BS : (m + 1) * BS
                            ]
                rhs = jnp.concatenate([tens[k, i, s] for s in range(S)], axis=1)
                for w in range(W):
                    lhs = jnp.concatenate([prod[0, w], prod[1, w]], axis=1)
                    put(i, w, dot_nt(lhs, rhs).astype(BF))
                return carry

            lax.fori_loop(0, 2, body, 0)

        def put_mid(i, w, r):
            win2[2 + i, w] = r

        def put_res(i, w, r):
            res[i, w] = r

        for g in (outer, inner):
            wait_env(g)
            swap_send(win1.at[pl.ds(2 + 2 * g, 2)], 0, g)
        for g in (inner, outer):
            wait_m(1, g)
            widen(0, win1, g)
            update(1, win1, g, put_mid)
            swap_send(win2.at[pl.ds(2 + 2 * g, 2)], 1, g)
        for g in (inner, outer):
            wait_m(0, g)
            widen(1, win2, g)
            update(0, win2, g, put_res)
            push(*out_args(g, right_out, 1))
        for g in (inner, outer):
            pushed(*out_args(g, right_out, 1))
        for k, win in ((0, win1), (1, win2)):
            for g in range(2):
                remote(
                    win.at[pl.ds(2 + 2 * g, 2)], land.at[k, 1 - g], x_send.at[k, g],
                    x_recv.at[k, 1 - g], up,
                ).wait_send()

    for t in range(2):
        pushed(*steps_args(t))
        pl.when(has_next[t])(lambda t=t: env_copy(t).wait_send())
        for k in range(2):
            pushed(*m_args(t, k))
    arrived(left_out.at[0], o_recv.at[0])
    arrived(right_out.at[0], o_recv.at[1])


def solution(mesh):
    zs = mesh.shape["site"] // 2

    def shards(site_tensors, charge_step, local_operator, left_boundary, right_boundary):
        steps = jnp.zeros((8, BS), jnp.int32).at[:2, :S].set(charge_step)
        op = jnp.zeros((R, BS), BF).at[:W, : W * S].set(local_operator.reshape(W, W * S))
        vmem = pl.BlockSpec(memory_space=pltpu.VMEM)
        anywhere = pl.BlockSpec(memory_space=pl.ANY)
        dma = pltpu.SemaphoreType.DMA
        env = (W, BS, BS)
        return pl.pallas_call(
            functools.partial(kernel, zs),
            out_shape=(
                jax.ShapeDtypeStruct(left_boundary.shape, BF),
                jax.ShapeDtypeStruct(right_boundary.shape, BF),
            ),
            in_specs=[vmem, vmem, anywhere, anywhere, anywhere],
            out_specs=(anywhere, anywhere),
            scratch_shapes=[
                pltpu.VMEM((2, 4, S, BS, BS), BF),
                pltpu.VMEM((8,) + env, BF),
                pltpu.VMEM((8,) + env, BF),
                pltpu.VMEM((2, 2, 2) + env, BF),
                pltpu.VMEM((2, 2, 2) + env, BF),
                pltpu.VMEM((4,) + env, BF),
                pltpu.VMEM((4,) + env, BF),
                pltpu.VMEM((2, W, BS, 2 * BS), BF),
                pltpu.VMEM((4, S) + env, BF),
                pltpu.VMEM((S, KW, KW), BF),
                pltpu.VMEM((5, S, BS, BS), BF),
                pltpu.VMEM((2, 8, BS), jnp.int32),
                pltpu.SMEM((8, BS), jnp.int32),
                dma((2,)),
                dma((2,)),
                dma((2, 2)),
                dma((2, 2)),
                dma((2,)),
                dma((2,)),
                dma((2, 2)),
                dma((2, 2)),
                dma((2,)),
                dma((2,)),
                dma,
            ],
            compiler_params=pltpu.CompilerParams(
                collective_id=0, has_side_effects=True, vmem_limit_bytes=52 * 2**20
            ),
        )(steps, op, site_tensors, left_boundary, right_boundary)

    placed = (
        P("site", "sector", None, None, None),
        P("site", None),
        P(),
        P("site", "sector", None, None, None),
        P("site", "sector", None, None, None),
    )
    return jax.shard_map(
        shards,
        mesh=mesh,
        in_specs=placed,
        out_specs=(P("site", "sector", None, None, None), P("site", "sector", None, None, None)),
        check_vma=False,
    )
```

```python
import functools

import jax
import jax.numpy as jnp
from jax import lax
from jax.experimental import pallas as pl
from jax.experimental.pallas import tpu as pltpu
from jax.sharding import PartitionSpec as P

MESH = pl.DeviceIdType.MESH
BF = jnp.bfloat16
F32 = jnp.float32
W = 13
S = 4
BS = 128
R = 16
KW = W * R


def dot(a, b):
    return jnp.dot(a, b, preferred_element_type=F32)


def dot_nt(a, b):
    return lax.dot_general(a, b, (((1,), (1,)), ((), ())), preferred_element_type=F32)


def kernel(
    zs, steps_in, op_ref, m_in, left_in, right_in, left_out, right_out,
    tens, win1, win2, land, shr, res, own, relay, prod, mix, kron, mt, op_v, steps_h, steps_v, steps_s,
    st_send, st_recv, m_send, m_recv, e_send, e_recv, r_send, r_recv, x_send, x_recv, o_send, o_recv, loc,
):
    site = lax.axis_index("site")
    sector = lax.axis_index("sector")
    z, c = site // 2, site % 2
    y, x = sector // 4, sector % 4
    half = x // 2
    slot = x % 2
    home = half == c
    is_right = (x == 0) | (x == 3)
    is_left = jnp.logical_not(is_right)

    def dev(zz, cc, yy, xx):
        return (zz * 2 + cc, yy * 4 + xx)

    def signal(sem, target):
        pl.semaphore_signal(sem, inc=1, device_id=target, device_id_type=MESH)

    left_task = dev(z, half, y, 1 + c)
    right_task = dev(z, half, y, 3 * c)
    left_near, left_far = c == 0, (c == 1) & (z + 1 < zs)
    right_near, right_far = c == 1, (c == 0) & (z >= 1)
    left_next = dev(z, half, y, 2)
    right_next = dev(z, half, y, 0)
    left_step = dev(z + 1, half, y, x)
    right_step = dev(z - 1, half, y, x)
    left_via = home & (z >= 1)
    right_via = home & (z + 1 < zs)
    left_last = dev(z, half, y, 1)
    right_last = dev(z, half, y, 3)
    left_from = dev(z - 1, 1, y, x)
    right_from = dev(z + 1, 0, y, x)
    src = [dev(z, half, y, 2 * c + k) for k in range(2)]
    away = half - 1 + is_right.astype(jnp.int32)
    fed = (z + away >= 0) & (z + away < zs)
    near = away == 0
    env_src = [dev(z, jnp.where(near, 1 - half, c), y, 2 * c + k) for k in range(2)]
    down = dev(z, 1 - c, (y + c + 3) % 4, x)
    up = dev(z, 1 - c, (y + c) % 4, x)

    steps_h[...] = jnp.zeros((8, BS), jnp.int32)
    steps_h[0:2, 0:S] = steps_in[...]

    barrier = pltpu.get_barrier_semaphore()
    for k in range(2):
        pl.when(jnp.logical_not(home & (slot == k)))(functools.partial(signal, barrier, src[k]))
        pl.when(fed & (near | (x != 2 * c + k)))(functools.partial(signal, barrier, env_src[k]))
    pl.when(x != 1 + c)(functools.partial(signal, barrier, left_task))
    pl.when(x != 3 * c)(functools.partial(signal, barrier, right_task))
    pl.when(left_via)(functools.partial(signal, barrier, left_from))
    pl.when(right_via)(functools.partial(signal, barrier, right_from))
    signal(barrier, down)
    signal(barrier, up)
    pl.semaphore_wait(
        barrier,
        7
        - 2 * home.astype(jnp.int32)
        + (left_far | right_far).astype(jnp.int32)
        + (left_via & (x != 1)).astype(jnp.int32)
        + (right_via & (x != 3)).astype(jnp.int32),
    )

    def remote(a, b, ss, rs, target):
        return pltpu.make_async_remote_copy(
            src_ref=a, dst_ref=b, send_sem=ss, recv_sem=rs, device_id=target, device_id_type=MESH
        )

    def push(a, b, ss, rs, target, here):
        @pl.when(here)
        def _():
            pltpu.make_async_copy(a, b, rs).start()

        @pl.when(jnp.logical_not(here))
        def _():
            remote(a, b, ss, rs, target).start()

    def pushed(a, b, ss, rs, target, here):
        @pl.when(jnp.logical_not(here))
        def _():
            remote(a, b, ss, rs, target).wait_send()

    def arrived(b, rs):
        pltpu.make_async_copy(b, b, rs).wait()

    tasks = ((left_task, x == 1 + c), (right_task, x == 3 * c))

    def steps_args(t):
        return (steps_h, steps_v.at[slot], st_send.at[t], st_recv.at[slot]) + tasks[t]

    def m_args(t, k):
        return (
            m_in.at[k], tens.at[k, pl.ds(2 * slot, 2)], m_send.at[t, k], m_recv.at[k, slot]
        ) + tasks[t]

    def near_copy(t, n):
        held, target = ((left_in, left_next), (right_in, right_next))[t]
        return remote(
            held.at[0, n], win1.at[2 + 2 * slot + n], e_send.at[t, n], e_recv.at[slot, n], target
        )

    def far_copy(t, n):
        held, target = ((left_in, left_step), (right_in, right_step))[t]
        return remote(
            held.at[0, n], relay.at[t, n], e_send.at[t, n], r_recv.at[t, n], target
        )

    def via_args(t, n):
        return (
            relay.at[t, n], win1.at[2 + 2 * slot + n], r_send.at[t, n], e_recv.at[slot, n],
            (left_last, right_last)[t], x == (1, 3)[t],
        )

    envs = ((left_near, left_far, left_via), (right_near, right_far, right_via))

    def env_ends(t, n):
        pl.when(envs[t][0])(lambda: near_copy(t, n).wait_send())
        pl.when(envs[t][1])(lambda: far_copy(t, n).wait_send())
        pl.when(envs[t][2])(lambda: pushed(*via_args(t, n)))

    for n in range(2):
        for t in range(2):
            pl.when(envs[t][1])(lambda t=t, n=n: far_copy(t, n).start())
            pl.when(envs[t][0] & is_right)(lambda t=t, n=n: near_copy(t, n).start())
    for t in range(2):
        push(*steps_args(t))
    for t in range(2):
        push(*m_args(t, t))

    @pl.when(jnp.logical_not(fed))
    def _():
        win1[2:6] = jnp.zeros((4, W, BS, BS), BF)

    op_v[...] = jnp.zeros((64, BS), F32)
    for w in range(W):
        op_v[S * w : S * w + S, 0:W] = op_ref[w].astype(F32)
    terms = op_v[...].astype(BF)
    rows = lax.broadcasted_iota(jnp.int32, (KW, BS), 0)
    cols = lax.broadcasted_iota(jnp.int32, (KW, BS), 1)
    spread = (rows // R == cols).astype(F32).astype(BF)
    rows = lax.broadcasted_iota(jnp.int32, (KW, 64), 0)
    cols = lax.broadcasted_iota(jnp.int32, (KW, 64), 1)
    place_row = lax.broadcasted_iota(jnp.int32, (KW, KW), 0) % R
    place_col = lax.broadcasted_iota(jnp.int32, (KW, KW), 1) % R
    for s in range(S):
        pick = ((rows // R) * S + s == cols).astype(F32).astype(BF)
        by_row = dot(pick, terms).astype(BF)

        @pl.when(is_left)
        def _():
            full = dot_nt(spread, by_row)
            kron[s] = jnp.where(place_row == place_col, full, 0.0).astype(BF)

        @pl.when(is_right)
        def _():
            full = dot_nt(by_row, spread)
            kron[s] = jnp.where(place_row == place_col, full, 0.0).astype(BF)

    for k in range(2):
        arrived(steps_v.at[k], st_recv.at[k])
    fetch = pltpu.make_async_copy(steps_v.at[0], steps_s, loc)
    fetch.start()
    fetch.wait()

    outer = c
    inner = 1 - c

    def wait_env(g):
        @pl.when(fed)
        def _():
            for n in range(2):
                arrived(win1.at[2 + 2 * g + n], e_recv.at[g, n])

    def wait_m(k, g):
        arrived(tens.at[k, pl.ds(2 * g, 2)], m_recv.at[k, g])

    def swap_copy(a, k, g, n, target):
        return remote(
            a, land.at[k, 1 - g, n], x_send.at[k, g, n], x_recv.at[k, 1 - g, n], target
        )

    def swap_send(a, k, g, n):
        pl.when(g == 0)(lambda: swap_copy(a, k, 0, n, down).start())
        pl.when(g == 1)(lambda: swap_copy(a, k, 1, n, up).start())

    def wait_land(k, g, n):
        arrived(land.at[k, g, n], x_recv.at[k, g, n])

    def out_args(g, n, target_ref, t):
        here = home & (slot == g)
        return (
            res.at[2 * g + n], target_ref.at[0, n], o_send.at[g, n], o_recv.at[t, n],
            dev(z, half, y, 2 * c + g), here,
        )

    def edge_first():
        for n in range(2):
            swap_send(win1.at[2 + 2 * outer + n], 0, outer, n)

    @pl.when(x == 0)
    def _():
        wait_env(outer)
        edge_first()

    @pl.when(is_left)
    def _():
        for t in range(2):
            pushed(*m_args(t, t))
        for n in range(2):
            for t in range(2):
                pl.when(envs[t][0])(lambda t=t, n=n: near_copy(t, n).start())

    for n in range(2):
        for t in range(2):

            @pl.when(envs[t][2])
            def _():
                arrived(relay.at[t, n], r_recv.at[t, n])
                push(*via_args(t, n))

    def later_tensors():
        for t in range(2):
            push(*m_args(t, 1 - t))

    def blend(load, store):
        for s in range(S):
            for a in range(0, BS // R, 2):
                both = jnp.concatenate([load(s, a), load(s, a + 1)], axis=1)
                r = dot(kron[s], both).astype(BF)
                store(s, a, r[:, :BS].reshape(W, R, BS))
                store(s, a + 1, r[:, BS:].reshape(W, R, BS))

    @pl.when(is_left)
    def _():
        mt[4] = jnp.zeros((S, BS, BS), BF)

        def flip(k, g):
            def body(n, carry):
                i = 2 * g + n
                for s in range(S):
                    mt[i, s] = tens[k, i, s].astype(F32).T.astype(BF)
                return carry

            lax.fori_loop(0, 2, body, 0)

        def expand(k, win, g):
            def body(n, carry):
                i = 2 * g + n
                for p in range(2):
                    m = jnp.concatenate([tens[k, i, 2 * p], tens[k, i, 2 * p + 1]], axis=1)
                    r = dot(win[2 + i].reshape(W * BS, BS), m).astype(BF)
                    prod[p] = r.reshape(W, BS, 2 * BS)

                def load(s, a):
                    block = prod[s // 2, :, a * R : (a + 1) * R, (s % 2) * BS : (s % 2 + 1) * BS]
                    return block.reshape(KW, BS)

                def store(s, a, r):
                    mix[i, s, :, a * R : (a + 1) * R, :] = r

                blend(load, store)
                return carry

            lax.fori_loop(0, 2, body, 0)

        def reach(k, j, low, high, put):
            origin = [j - steps_s[k, s] for s in range(S)]
            inside = [(i >= low) & (i <= high) for i in origin]
            clipped = [jnp.minimum(jnp.maximum(i, low), high) for i in origin]
            lhs = jnp.concatenate(
                [mt[jnp.where(inside[s], clipped[s], 4), s] for s in range(S)], axis=1
            )
            for v0 in range(0, W, 2):
                vs = range(v0, min(v0 + 2, W))
                rhs = jnp.concatenate(
                    [
                        jnp.concatenate([mix[clipped[s], s, v] for s in range(S)], axis=0)
                        for v in vs
                    ],
                    axis=1,
                )
                r = dot(lhs, rhs).astype(BF)
                for n, v in enumerate(vs):
                    put(v, r[:, n * BS : (n + 1) * BS])

        def share(k, g):
            for n in range(2):

                def put(v, r):
                    shr[k, g, n, v] = r

                reach(k, 6 * g - 2 + n, 2 * g, 2 * g + 1, put)
                swap_send(shr.at[k, g, n], k, g, n)

        def settle(k):
            def body(j, carry):
                def put(v, r):
                    own[j, v] = r

                reach(k, j, 0, 3, put)
                return carry

            lax.fori_loop(0, 4, body, 0)

        def join(k, g, n):
            wait_land(k, g, n)
            j = 2 * g + n

            def body(v, carry):
                r = (own[j, v].astype(F32) + land[k, g, n, v].astype(F32)).astype(BF)
                if k == 0:
                    win2[2 + j, v] = r
                else:
                    res[j, v] = r
                return carry

            lax.fori_loop(0, W, body, 0)

        for first, g in ((True, outer), (False, inner)):
            wait_m(0, g)
            flip(0, g)
            wait_env(g)
            expand(0, win1, g)
            if not first:
                later_tensors()
            share(0, g)
        settle(0)
        for g in (outer, inner):
            wait_m(1, g)
            flip(1, g)
            for n in range(2):
                join(0, g, n)
            expand(1, win2, g)
            share(1, g)
        settle(1)
        for g in (inner, outer):
            for n in range(2):
                join(1, g, n)
                push(*out_args(g, n, left_out, 0))
        for g in range(2):
            for n in range(2):
                pushed(*out_args(g, n, left_out, 0))
                for k in range(2):
                    swap_copy(shr.at[k, g, n], k, g, n, up).wait_send()

    @pl.when(is_right)
    def _():
        def widen(k, win, g):
            for n in range(2):
                wait_land(k, g, n)
                win[6 * g + n] = land[k, g, n]

        def update(k, win, g, n, put):
            def body(n, carry):
                i = 2 * g + n
                at = [2 + i + steps_s[k, s] for s in range(S)]

                def load(s, a):
                    return win[at[s], :, a * R : (a + 1) * R, :].reshape(KW, BS)

                def store(s, a, r):
                    mix[0, s, :, a * R : (a + 1) * R, :] = r

                blend(load, store)
                for s in range(S):
                    for w0 in range(0, W, 2):
                        ws = range(w0, min(w0 + 2, W))
                        rhs = jnp.concatenate([mix[0, s, w] for w in ws], axis=1)
                        r = dot(tens[k, i, s], rhs).astype(BF)
                        for m, w in enumerate(ws):
                            prod[s // 2, w, :, (s % 2) * BS : (s % 2 + 1) * BS] = r[
                                :, m * BS : (m + 1) * BS
                            ]
                rhs = jnp.concatenate([tens[k, i, s] for s in range(S)], axis=1)
                for w in range(W):
                    lhs = jnp.concatenate([prod[0, w], prod[1, w]], axis=1)
                    put(i, w, dot_nt(lhs, rhs).astype(BF))

            body(n, 0)

        def put_mid(i, w, r):
            win2[2 + i, w] = r

        def put_res(i, w, r):
            res[i, w] = r

        @pl.when(x == 3)
        def _():
            wait_env(outer)
            edge_first()

        wait_env(inner)
        for n in range(2):
            swap_send(win1.at[2 + 2 * inner + n], 0, inner, n)
        for first, g in ((True, outer), (False, inner)):
            wait_m(1, g)
            if first:
                later_tensors()
            widen(0, win1, g)
            for n in range(2):
                update(1, win1, g, n, put_mid)
                swap_send(win2.at[2 + 2 * g + n], 1, g, n)
        for g in (inner, outer):
            wait_m(0, g)
            widen(1, win2, g)
            for n in range(2):
                update(0, win2, g, n, put_res)
                push(*out_args(g, n, right_out, 1))
        for g in range(2):
            for n in range(2):
                pushed(*out_args(g, n, right_out, 1))
                for k, win in ((0, win1), (1, win2)):
                    swap_copy(win.at[2 + 2 * g + n], k, g, n, up).wait_send()

    for t in range(2):
        pushed(*steps_args(t))
        pl.when(is_right)(lambda t=t: pushed(*m_args(t, t)))
        pushed(*m_args(t, 1 - t))
        for n in range(2):
            env_ends(t, n)
    for n in range(2):
        arrived(left_out.at[0, n], o_recv.at[0, n])
        arrived(right_out.at[0, n], o_recv.at[1, n])


def solution(mesh):
    zs = mesh.shape["site"] // 2

    def shards(site_tensors, charge_step, local_operator, left_boundary, right_boundary):
        op = local_operator.transpose(0, 2, 1)
        vmem = pl.BlockSpec(memory_space=pltpu.VMEM)
        anywhere = pl.BlockSpec(memory_space=pl.ANY)
        dma = pltpu.SemaphoreType.DMA
        env = (W, BS, BS)
        return pl.pallas_call(
            functools.partial(kernel, zs),
            out_shape=(
                jax.ShapeDtypeStruct(left_boundary.shape, BF),
                jax.ShapeDtypeStruct(right_boundary.shape, BF),
            ),
            in_specs=[vmem, vmem, anywhere, anywhere, anywhere],
            out_specs=(anywhere, anywhere),
            scratch_shapes=[
                pltpu.VMEM((2, 4, S, BS, BS), BF),
                pltpu.VMEM((8,) + env, BF),
                pltpu.VMEM((8,) + env, BF),
                pltpu.VMEM((2, 2, 2) + env, BF),
                pltpu.VMEM((2, 2, 2) + env, BF),
                pltpu.VMEM((4,) + env, BF),
                pltpu.VMEM((4,) + env, BF),
                pltpu.VMEM((2, 2) + env, BF),
                pltpu.VMEM((2, W, BS, 2 * BS), BF),
                pltpu.VMEM((4, S) + env, BF),
                pltpu.VMEM((S, KW, KW), BF),
                pltpu.VMEM((5, S, BS, BS), BF),
                pltpu.VMEM((64, BS), F32),
                pltpu.VMEM((8, BS), jnp.int32),
                pltpu.VMEM((2, 8, BS), jnp.int32),
                pltpu.SMEM((8, BS), jnp.int32),
                dma((2,)),
                dma((2,)),
                dma((2, 2)),
                dma((2, 2)),
                dma((2, 2)),
                dma((2, 2)),
                dma((2, 2)),
                dma((2, 2)),
                dma((2, 2, 2)),
                dma((2, 2, 2)),
                dma((2, 2)),
                dma((2, 2)),
                dma,
            ],
            compiler_params=pltpu.CompilerParams(
                collective_id=0, has_side_effects=True, vmem_limit_bytes=62 * 2**20
            ),
        )(charge_step, op, site_tensors, left_boundary, right_boundary)

    placed = (
        P("site", "sector", None, None, None),
        P("site", None),
        P(),
        P("site", "sector", None, None, None),
        P("site", "sector", None, None, None),
    )
    return jax.shard_map(
        shards,
        mesh=mesh,
        in_specs=placed,
        out_specs=(P("site", "sector", None, None, None), P("site", "sector", None, None, None)),
        check_vma=False,
    )
```

```python
import functools

import jax
import jax.numpy as jnp
from jax import lax
from jax.experimental import pallas as pl
from jax.experimental.pallas import tpu as pltpu
from jax.sharding import PartitionSpec as P

MESH = pl.DeviceIdType.MESH
BF = jnp.bfloat16
F32 = jnp.float32
W = 13
S = 4
BS = 128
R = 16
KW = W * R


def dot(a, b):
    return jnp.dot(a, b, preferred_element_type=F32)


def dot_nt(a, b):
    return lax.dot_general(a, b, (((1,), (1,)), ((), ())), preferred_element_type=F32)


def kernel(
    zs, steps_in, op_ref, m_in, left_in, right_in, left_out, right_out,
    tens, win1, win2, land, shr, res, own, relay, prod, mix, kron, mt, op_v, steps_h, steps_v, steps_s,
    st_send, st_recv, m_send, m_recv, e_send, e_recv, r_send, r_recv, x_send, x_recv, o_send, o_recv, loc,
):
    site = lax.axis_index("site")
    sector = lax.axis_index("sector")
    z, c = site // 2, site % 2
    y, x = sector // 4, sector % 4
    half = x // 2
    slot = x % 2
    home = half == c
    is_right = (x == 0) | (x == 3)
    is_left = jnp.logical_not(is_right)

    def dev(zz, cc, yy, xx):
        return (zz * 2 + cc, yy * 4 + xx)

    def signal(sem, target):
        pl.semaphore_signal(sem, inc=1, device_id=target, device_id_type=MESH)

    left_task = dev(z, half, y, 1 + c)
    right_task = dev(z, half, y, 3 * c)
    left_near, left_far = c == 0, (c == 1) & (z + 1 < zs)
    right_near, right_far = c == 1, (c == 0) & (z >= 1)
    left_next = dev(z, half, y, 2)
    right_next = dev(z, half, y, 0)
    left_step = dev(z + 1, half, y, x)
    right_step = dev(z - 1, half, y, x)
    left_via = home & (z >= 1)
    right_via = home & (z + 1 < zs)
    left_last = dev(z, half, y, 1)
    right_last = dev(z, half, y, 3)
    left_from = dev(z - 1, 1, y, x)
    right_from = dev(z + 1, 0, y, x)
    src = [dev(z, half, y, 2 * c + k) for k in range(2)]
    away = half - 1 + is_right.astype(jnp.int32)
    fed = (z + away >= 0) & (z + away < zs)
    near = away == 0
    env_src = [dev(z, jnp.where(near, 1 - half, c), y, 2 * c + k) for k in range(2)]
    down = dev(z, 1 - c, (y + c + 3) % 4, x)
    up = dev(z, 1 - c, (y + c) % 4, x)

    steps_h[...] = jnp.zeros((8, BS), jnp.int32)
    steps_h[0:2, 0:S] = steps_in[...]

    barrier = pltpu.get_barrier_semaphore()
    for k in range(2):
        pl.when(jnp.logical_not(home & (slot == k)))(functools.partial(signal, barrier, src[k]))
        pl.when(fed & (near | (x != 2 * c + k)))(functools.partial(signal, barrier, env_src[k]))
    pl.when(x != 1 + c)(functools.partial(signal, barrier, left_task))
    pl.when(x != 3 * c)(functools.partial(signal, barrier, right_task))
    pl.when(left_via)(functools.partial(signal, barrier, left_from))
    pl.when(right_via)(functools.partial(signal, barrier, right_from))
    signal(barrier, down)
    signal(barrier, up)
    pl.semaphore_wait(
        barrier,
        7
        - 2 * home.astype(jnp.int32)
        + (left_far | right_far).astype(jnp.int32)
        + (left_via & (x != 1)).astype(jnp.int32)
        + (right_via & (x != 3)).astype(jnp.int32),
    )

    def remote(a, b, ss, rs, target):
        return pltpu.make_async_remote_copy(
            src_ref=a, dst_ref=b, send_sem=ss, recv_sem=rs, device_id=target, device_id_type=MESH
        )

    def push(a, b, ss, rs, target, here):
        @pl.when(here)
        def _():
            pltpu.make_async_copy(a, b, rs).start()

        @pl.when(jnp.logical_not(here))
        def _():
            remote(a, b, ss, rs, target).start()

    def pushed(a, b, ss, rs, target, here):
        @pl.when(jnp.logical_not(here))
        def _():
            remote(a, b, ss, rs, target).wait_send()

    def arrived(b, rs):
        pltpu.make_async_copy(b, b, rs).wait()

    tasks = ((left_task, x == 1 + c), (right_task, x == 3 * c))

    def steps_args(t):
        return (steps_h, steps_v.at[slot], st_send.at[t], st_recv.at[slot]) + tasks[t]

    def m_args(t, k):
        return (
            m_in.at[k], tens.at[k, pl.ds(2 * slot, 2)], m_send.at[t, k], m_recv.at[k, slot]
        ) + tasks[t]

    def near_copy(t, n):
        held, target = ((left_in, left_next), (right_in, right_next))[t]
        return remote(
            held.at[0, n], win1.at[2 + 2 * slot + n], e_send.at[t, n], e_recv.at[slot, n], target
        )

    def far_copy(t, n):
        held, target = ((left_in, left_step), (right_in, right_step))[t]
        return remote(
            held.at[0, n], relay.at[t, n], e_send.at[t, n], r_recv.at[t, n], target
        )

    def via_args(t, n):
        return (
            relay.at[t, n], win1.at[2 + 2 * slot + n], r_send.at[t, n], e_recv.at[slot, n],
            (left_last, right_last)[t], x == (1, 3)[t],
        )

    envs = ((left_near, left_far, left_via), (right_near, right_far, right_via))

    def env_ends(t, n):
        pl.when(envs[t][0])(lambda: near_copy(t, n).wait_send())
        pl.when(envs[t][1])(lambda: far_copy(t, n).wait_send())
        pl.when(envs[t][2])(lambda: pushed(*via_args(t, n)))

    for n in range(2):
        for t in range(2):
            pl.when(envs[t][1])(lambda t=t, n=n: far_copy(t, n).start())
            pl.when(envs[t][0] & is_right)(lambda t=t, n=n: near_copy(t, n).start())
    for t in range(2):
        push(*steps_args(t))
    for t in range(2):
        push(*m_args(t, t))

    @pl.when(jnp.logical_not(fed))
    def _():
        win1[2:6] = jnp.zeros((4, W, BS, BS), BF)

    op_v[...] = jnp.zeros((64, BS), F32)
    for w in range(W):
        op_v[S * w : S * w + S, 0:W] = op_ref[w].astype(F32)
    terms = op_v[...].astype(BF)
    rows = lax.broadcasted_iota(jnp.int32, (KW, BS), 0)
    cols = lax.broadcasted_iota(jnp.int32, (KW, BS), 1)
    spread = (rows // R == cols).astype(F32).astype(BF)
    rows = lax.broadcasted_iota(jnp.int32, (KW, 64), 0)
    cols = lax.broadcasted_iota(jnp.int32, (KW, 64), 1)
    place_row = lax.broadcasted_iota(jnp.int32, (KW, KW), 0) % R
    place_col = lax.broadcasted_iota(jnp.int32, (KW, KW), 1) % R
    for s in range(S):
        pick = ((rows // R) * S + s == cols).astype(F32).astype(BF)
        by_row = dot(pick, terms).astype(BF)

        @pl.when(is_left)
        def _():
            full = dot_nt(spread, by_row)
            kron[s] = jnp.where(place_row == place_col, full, 0.0).astype(BF)

        @pl.when(is_right)
        def _():
            full = dot_nt(by_row, spread)
            kron[s] = jnp.where(place_row == place_col, full, 0.0).astype(BF)

    for k in range(2):
        arrived(steps_v.at[k], st_recv.at[k])
    fetch = pltpu.make_async_copy(steps_v.at[0], steps_s, loc)
    fetch.start()
    fetch.wait()

    outer = c
    inner = 1 - c

    def wait_env(g):
        @pl.when(fed)
        def _():
            for n in range(2):
                arrived(win1.at[2 + 2 * g + n], e_recv.at[g, n])

    def wait_m(k, g):
        arrived(tens.at[k, pl.ds(2 * g, 2)], m_recv.at[k, g])

    def swap_copy(a, k, g, n, target):
        return remote(
            a, land.at[k, 1 - g, n], x_send.at[k, g, n], x_recv.at[k, 1 - g, n], target
        )

    def swap_send(a, k, g, n):
        pl.when(g == 0)(lambda: swap_copy(a, k, 0, n, down).start())
        pl.when(g == 1)(lambda: swap_copy(a, k, 1, n, up).start())

    def wait_land(k, g, n):
        arrived(land.at[k, g, n], x_recv.at[k, g, n])

    def out_args(g, n, target_ref, t):
        here = home & (slot == g)
        return (
            res.at[2 * g + n], target_ref.at[0, n], o_send.at[g, n], o_recv.at[t, n],
            dev(z, half, y, 2 * c + g), here,
        )

    def edge_first():
        for n in range(2):
            swap_send(win1.at[2 + 2 * outer + n], 0, outer, n)

    @pl.when(x == 0)
    def _():
        wait_env(outer)
        edge_first()

    @pl.when(is_left)
    def _():
        for t in range(2):
            pushed(*m_args(t, t))
        for n in range(2):
            for t in range(2):
                pl.when(envs[t][0])(lambda t=t, n=n: near_copy(t, n).start())

    for n in range(2):
        for t in range(2):

            @pl.when(envs[t][2])
            def _():
                arrived(relay.at[t, n], r_recv.at[t, n])
                push(*via_args(t, n))

    def later_tensors():
        for t in range(2):
            push(*m_args(t, 1 - t))

    def blend(load, store):
        for s in range(S):
            for a in range(0, BS // R, 2):
                both = jnp.concatenate([load(s, a), load(s, a + 1)], axis=1)
                r = dot(kron[s], both).astype(BF)
                store(s, a, r[:, :BS].reshape(W, R, BS))
                store(s, a + 1, r[:, BS:].reshape(W, R, BS))

    @pl.when(is_left)
    def _():
        mt[4] = jnp.zeros((S, BS, BS), BF)

        def flip(k, g):
            def body(n, carry):
                i = 2 * g + n
                for s in range(S):
                    mt[i, s] = tens[k, i, s].astype(F32).T.astype(BF)
                return carry

            lax.fori_loop(0, 2, body, 0)

        def expand(k, win, g):
            def body(n, carry):
                i = 2 * g + n
                for p in range(2):
                    m = jnp.concatenate([tens[k, i, 2 * p], tens[k, i, 2 * p + 1]], axis=1)
                    r = dot(win[2 + i].reshape(W * BS, BS), m).astype(BF)
                    prod[p] = r.reshape(W, BS, 2 * BS)

                def load(s, a):
                    block = prod[s // 2, :, a * R : (a + 1) * R, (s % 2) * BS : (s % 2 + 1) * BS]
                    return block.reshape(KW, BS)

                def store(s, a, r):
                    mix[i, s, :, a * R : (a + 1) * R, :] = r

                blend(load, store)
                return carry

            lax.fori_loop(0, 2, body, 0)

        def reach(k, j, low, high, put):
            origin = [j - steps_s[k, s] for s in range(S)]
            inside = [(i >= low) & (i <= high) for i in origin]
            clipped = [jnp.minimum(jnp.maximum(i, low), high) for i in origin]
            lhs = jnp.concatenate(
                [mt[jnp.where(inside[s], clipped[s], 4), s] for s in range(S)], axis=1
            )
            for v0 in range(0, W, 2):
                vs = range(v0, min(v0 + 2, W))
                rhs = jnp.concatenate(
                    [
                        jnp.concatenate([mix[clipped[s], s, v] for s in range(S)], axis=0)
                        for v in vs
                    ],
                    axis=1,
                )
                r = dot(lhs, rhs).astype(BF)
                for n, v in enumerate(vs):
                    put(v, r[:, n * BS : (n + 1) * BS])

        def share(k, g):
            for n in range(2):

                def put(v, r):
                    shr[k, g, n, v] = r

                reach(k, 6 * g - 2 + n, 2 * g, 2 * g + 1, put)
                swap_send(shr.at[k, g, n], k, g, n)

        def settle(k):
            def body(j, carry):
                def put(v, r):
                    own[j, v] = r

                reach(k, j, 0, 3, put)
                return carry

            lax.fori_loop(0, 4, body, 0)

        def join(k, g, n):
            wait_land(k, g, n)
            j = 2 * g + n

            def body(v, carry):
                r = (own[j, v].astype(F32) + land[k, g, n, v].astype(F32)).astype(BF)
                if k == 0:
                    win2[2 + j, v] = r
                else:
                    res[j, v] = r
                return carry

            lax.fori_loop(0, W, body, 0)

        for first, g in ((True, outer), (False, inner)):
            wait_m(0, g)
            flip(0, g)
            wait_env(g)
            expand(0, win1, g)
            share(0, g)
            if first:
                later_tensors()
        settle(0)
        for g in (outer, inner):
            wait_m(1, g)
            flip(1, g)
            for n in range(2):
                join(0, g, n)
            expand(1, win2, g)
            share(1, g)
        settle(1)
        for g in (inner, outer):
            for n in range(2):
                join(1, g, n)
                push(*out_args(g, n, left_out, 0))
        for g in range(2):
            for n in range(2):
                pushed(*out_args(g, n, left_out, 0))
                for k in range(2):
                    swap_copy(shr.at[k, g, n], k, g, n, up).wait_send()

    @pl.when(is_right)
    def _():
        def widen(k, win, g):
            for n in range(2):
                wait_land(k, g, n)
                win[6 * g + n] = land[k, g, n]

        def update(k, win, g, n, put):
            def body(n, carry):
                i = 2 * g + n
                at = [2 + i + steps_s[k, s] for s in range(S)]

                def load(s, a):
                    return win[at[s], :, a * R : (a + 1) * R, :].reshape(KW, BS)

                def store(s, a, r):
                    mix[0, s, :, a * R : (a + 1) * R, :] = r

                blend(load, store)
                for s in range(S):
                    for w0 in range(0, W, 2):
                        ws = range(w0, min(w0 + 2, W))
                        rhs = jnp.concatenate([mix[0, s, w] for w in ws], axis=1)
                        r = dot(tens[k, i, s], rhs).astype(BF)
                        for m, w in enumerate(ws):
                            prod[s // 2, w, :, (s % 2) * BS : (s % 2 + 1) * BS] = r[
                                :, m * BS : (m + 1) * BS
                            ]
                rhs = jnp.concatenate([tens[k, i, s] for s in range(S)], axis=1)
                for w in range(W):
                    lhs = jnp.concatenate([prod[0, w], prod[1, w]], axis=1)
                    put(i, w, dot_nt(lhs, rhs).astype(BF))

            body(n, 0)

        def put_mid(i, w, r):
            win2[2 + i, w] = r

        def put_res(i, w, r):
            res[i, w] = r

        @pl.when(x == 3)
        def _():
            wait_env(outer)
            edge_first()

        wait_env(inner)
        for n in range(2):
            swap_send(win1.at[2 + 2 * inner + n], 0, inner, n)
        for first, g in ((True, outer), (False, inner)):
            wait_m(1, g)
            if first:
                later_tensors()
            widen(0, win1, g)
            for n in range(2):
                update(1, win1, g, n, put_mid)
                swap_send(win2.at[2 + 2 * g + n], 1, g, n)
        for g in (inner, outer):
            wait_m(0, g)
            widen(1, win2, g)
            for n in range(2):
                update(0, win2, g, n, put_res)
                push(*out_args(g, n, right_out, 1))
        for g in range(2):
            for n in range(2):
                pushed(*out_args(g, n, right_out, 1))
                for k, win in ((0, win1), (1, win2)):
                    swap_copy(win.at[2 + 2 * g + n], k, g, n, up).wait_send()

    for t in range(2):
        pushed(*steps_args(t))
        pl.when(is_right)(lambda t=t: pushed(*m_args(t, t)))
        pushed(*m_args(t, 1 - t))
        for n in range(2):
            env_ends(t, n)
    for n in range(2):
        arrived(left_out.at[0, n], o_recv.at[0, n])
        arrived(right_out.at[0, n], o_recv.at[1, n])


def solution(mesh):
    zs = mesh.shape["site"] // 2

    def shards(site_tensors, charge_step, local_operator, left_boundary, right_boundary):
        op = local_operator.transpose(0, 2, 1)
        vmem = pl.BlockSpec(memory_space=pltpu.VMEM)
        anywhere = pl.BlockSpec(memory_space=pl.ANY)
        dma = pltpu.SemaphoreType.DMA
        env = (W, BS, BS)
        return pl.pallas_call(
            functools.partial(kernel, zs),
            out_shape=(
                jax.ShapeDtypeStruct(left_boundary.shape, BF),
                jax.ShapeDtypeStruct(right_boundary.shape, BF),
            ),
            in_specs=[vmem, vmem, anywhere, anywhere, anywhere],
            out_specs=(anywhere, anywhere),
            scratch_shapes=[
                pltpu.VMEM((2, 4, S, BS, BS), BF),
                pltpu.VMEM((8,) + env, BF),
                pltpu.VMEM((8,) + env, BF),
                pltpu.VMEM((2, 2, 2) + env, BF),
                pltpu.VMEM((2, 2, 2) + env, BF),
                pltpu.VMEM((4,) + env, BF),
                pltpu.VMEM((4,) + env, BF),
                pltpu.VMEM((2, 2) + env, BF),
                pltpu.VMEM((2, W, BS, 2 * BS), BF),
                pltpu.VMEM((4, S) + env, BF),
                pltpu.VMEM((S, KW, KW), BF),
                pltpu.VMEM((5, S, BS, BS), BF),
                pltpu.VMEM((64, BS), F32),
                pltpu.VMEM((8, BS), jnp.int32),
                pltpu.VMEM((2, 8, BS), jnp.int32),
                pltpu.SMEM((8, BS), jnp.int32),
                dma((2,)),
                dma((2,)),
                dma((2, 2)),
                dma((2, 2)),
                dma((2, 2)),
                dma((2, 2)),
                dma((2, 2)),
                dma((2, 2)),
                dma((2, 2, 2)),
                dma((2, 2, 2)),
                dma((2, 2)),
                dma((2, 2)),
                dma,
            ],
            compiler_params=pltpu.CompilerParams(
                collective_id=0, has_side_effects=True, vmem_limit_bytes=62 * 2**20
            ),
        )(charge_step, op, site_tensors, left_boundary, right_boundary)

    placed = (
        P("site", "sector", None, None, None),
        P("site", None),
        P(),
        P("site", "sector", None, None, None),
        P("site", "sector", None, None, None),
    )
    return jax.shard_map(
        shards,
        mesh=mesh,
        in_specs=placed,
        out_specs=(P("site", "sector", None, None, None), P("site", "sector", None, None, None)),
        check_vma=False,
    )
```
